256 devices in a mesh: dp: 16 (over z_hi, x, core), slot: 4 (over y), hid: 4 (over z_lo).
Axes of the slice: x: 4, y: 4, z: 8 (z_hi: 2, z_lo: 4; z = z_hi * 4 + z_lo), core: 2. Of those that a mesh axis runs over, the one named last changes fastest.
Arguments:
- master_weights: float32 [8, 3, 768, 2048], P('slot', None, 'hid', 'dp'), may hold values from -0.125 to 0.125
- first_moment: float32 [8, 3, 768, 2048], P('slot', None, 'hid', 'dp'), may hold values from -6 to 6
- second_moment: float32 [8, 3, 768, 2048], P('slot', None, 'hid', 'dp'), may hold values from 1 to 100
- tokens_one: bfloat16 [16384, 2048], P('dp'), may hold values from -6 to 6
- grad_out: bfloat16 [16384, 2048], P('dp'), may hold values from -6 to 6
- route_one: int32 [16384, 2], P('dp'), may hold values from 0 to 7, all different within a row
- prob_one: float32 [16384, 2], P('dp'), may hold values from 0.05 to 0.6
- tokens_two: bfloat16 [16384, 2048], P('dp'), may hold values from -6 to 6
- route_two: int32 [16384, 2], P('dp'), may hold values from 0 to 7, all different within a row
- prob_two: float32 [16384, 2], P('dp'), may hold values from 0.05 to 0.6
- old_order: int32 [8], replicated, may hold values from 0 to 7, each once
- new_order: int32 [8], replicated, may hold values from 0 to 7, each once
Outputs:
- moved_master: float32 [8, 3, 768, 2048], P('slot', None, 'hid', 'dp')
- moved_first: float32 [8, 3, 768, 2048], P('slot', None, 'hid', 'dp')
- moved_second: float32 [8, 3, 768, 2048], P('slot', None, 'hid', 'dp')
- next_output: bfloat16 [16384, 2048], P('dp', ('slot', 'hid'))
The draws below stay inside these ranges and needn't reach their ends.
Inputs may be any that keep to these rules, and one draw needn't show every extreme that they name: `old_order`: lists each of the 8 experts once. `new_order`: lists each of the 8 experts once. `route_one`: each row names 2 different experts. `route_two`: each row names 2 different experts.
All inputs are finite; a program needn't handle non-finite values.
Results may differ from the reference program's by a relative error of at most 0.017.
Values may be sent and summed in bfloat16 or wider, within the bound.
No kernel may reach another device: no remote copies, remote signals or barrier semaphores. Data moves between devices by JAX's collectives and lax.ppermute only.
A program may use at most 128 MiB of HBM per device.

```python
import math
import jax
import jax.numpy as jnp
from jax import lax

D = 2048
FF = 768
TOP = 2
EXPERTS = 8
TOKENS = 16384


def shard_levels(key, dims, cuts, smallest, high):
    gain = 1.0
    for dim, blocks in cuts:
        steps = jax.random.uniform(jax.random.fold_in(jax.random.fold_in(key, 6), dim), (blocks,), jnp.float32, smallest / len(cuts), high / len(cuts))
        gain = gain * jnp.repeat(jnp.exp(steps), dims[dim] // blocks).reshape((-1,) + (1,) * (len(dims) - 1 - dim))
    return gain


def choose_distinct(rng, rows, count, top, lift):
    order = jax.random.permutation(jax.random.fold_in(rng, 1), count)
    boost = order
    for power in range(3):
        boost = boost * boost // count
    boost = boost * lift // count
    lots = jax.random.randint(jax.random.fold_in(rng, 2), (rows, count), 0, 4096) + boost
    holders = jax.random.permutation(jax.random.fold_in(rng, 3), rows)[jnp.arange(count) % rows]
    lots = jnp.where(jnp.arange(rows)[:, None] == holders[None, :], 1 << 14, lots)
    priority = lots * count + jnp.arange(count)
    return lax.top_k(priority.astype(jnp.int32), top)[1].astype(jnp.int32)


def bell_draw(stream_key, dims, scale, limit, shards=(), held_as=jnp.bfloat16):
    drawn = scale * jax.random.normal(stream_key, dims, jnp.float32)
    if shards:
        drawn = drawn * shard_levels(stream_key, dims, shards, -0.22, 0.18)
    return jnp.clip(drawn, -limit, limit).astype(held_as)


def setup_inputs(seed: int = 0) -> dict:
    keys = jax.random.split(jax.random.key(seed), 13)
    return {
        "master_weights": bell_draw(keys[0], (EXPERTS, 3, FF, D), D ** -0.5, 0.125, ((0, 4), (2, 4), (3, 16)), jnp.float32),
        "first_moment": bell_draw(keys[1], (EXPERTS, 3, FF, D), 1.0, 6.0, ((0, 4), (2, 4), (3, 16)), jnp.float32),
        "second_moment": jnp.clip(jnp.exp(math.log(100.0) - 4.6051702 * jax.random.uniform(keys[2], (EXPERTS, 3, FF, D), jnp.float32) ** shard_levels(keys[2], (EXPERTS, 3, FF, D), ((0, 4), (2, 4), (3, 16)), -0.2, 0.2)), 1.0, 100.0),
        "tokens_one": bell_draw(keys[3], (TOKENS, D), 1.0, 6.0, ((0, 16),)),
        "grad_out": bell_draw(keys[4], (TOKENS, D), 1.0, 6.0, ((0, 16),)),
        "route_one": choose_distinct(keys[5], TOKENS, EXPERTS, TOP, 4096),
        "prob_one": jnp.clip(0.05 + 0.55 * jax.random.uniform(keys[6], (TOKENS, TOP), jnp.float32) ** shard_levels(keys[6], (TOKENS, TOP), ((0, 16),), -0.2, 0.2), 0.05, 0.6),
        "tokens_two": bell_draw(keys[7], (TOKENS, D), 1.0, 6.0, ((0, 16),)),
        "route_two": choose_distinct(keys[8], TOKENS, EXPERTS, TOP, 4096),
        "prob_two": jnp.clip(0.05 + 0.55 * jax.random.uniform(keys[9], (TOKENS, TOP), jnp.float32) ** shard_levels(keys[9], (TOKENS, TOP), ((0, 16),), -0.2, 0.2), 0.05, 0.6),
        "old_order": jax.random.permutation(keys[10], EXPERTS).astype(jnp.int32),
        "new_order": jax.random.permutation(keys[11], EXPERTS).astype(jnp.int32),
    }


learn_rate = 0.001
beta_one = 0.9
beta_two = 0.95
epsilon = 1e-08
decay_rate = 0.1

def rows_by(left, right):
    return lax.dot_general(left, right, (((1,), (1,)), ((), ())), preferred_element_type=jnp.float32)

def cols_by(left, right):
    return lax.dot_general(left, right, (((0,), (0,)), ((), ())), preferred_element_type=jnp.float32)

def expert_grads(tokens, grad_out, scaling, weights):
    gate_proj = rows_by(tokens, weights[0])
    up_proj = rows_by(tokens, weights[1])
    logistic = jax.nn.sigmoid(gate_proj)
    swish_gate = gate_proj * logistic
    activated = (swish_gate * up_proj).astype(jnp.bfloat16)
    scaled_grad = (scaling[:, None] * grad_out.astype(jnp.float32)).astype(jnp.bfloat16)
    d_down = cols_by(activated, scaled_grad)
    d_activated = rows_by(scaled_grad, weights[2])
    d_gate = (d_activated * up_proj * logistic * (1.0 + gate_proj * (1.0 - logistic))).astype(jnp.bfloat16)
    d_up = (d_activated * swish_gate).astype(jnp.bfloat16)
    return jnp.stack([cols_by(d_gate, tokens), cols_by(d_up, tokens), d_down])

def expert_out(tokens, scaling, weights):
    gate_proj = rows_by(tokens, weights[0])
    up_proj = rows_by(tokens, weights[1])
    mixed = (scaling[:, None] * gate_proj * jax.nn.sigmoid(gate_proj) * up_proj).astype(jnp.bfloat16)
    return jnp.dot(mixed, weights[2], preferred_element_type=jnp.float32)

def adamw_update(master, moment_a, moment_b, grad_sum):
    new_a = beta_one * moment_a + (1.0 - beta_one) * grad_sum
    new_b = beta_two * moment_b + (1.0 - beta_two) * grad_sum * grad_sum
    fixed_a = new_a / (1.0 - beta_one ** 10)
    fixed_b = new_b / (1.0 - beta_two ** 10)
    new_master = master - learn_rate * (fixed_a / (jnp.sqrt(fixed_b) + epsilon) + decay_rate * master)
    return (new_master, new_a, new_b)

def coefficient(routes, probs, expert):
    return lax.optimization_barrier(jnp.sum(jnp.where(routes == expert, probs, 0.0), axis=1))

def reference(master_weights, first_moment, second_moment, tokens_one, grad_out, route_one, prob_one, tokens_two, route_two, prob_two, old_order, new_order):
    weights = master_weights.astype(jnp.bfloat16)
    gradients = []
    for position in range(EXPERTS):
        scaling = coefficient(route_one, prob_one, old_order[position])
        gradients.append(expert_grads(tokens_one, grad_out, scaling, weights[position]))
    gradients = jnp.stack(gradients)
    new_master, new_a, new_b = adamw_update(master_weights, first_moment, second_moment, gradients)
    positions = jnp.arange(EXPERTS, dtype=jnp.int32)
    source = lax.optimization_barrier(jnp.sum(jnp.where(old_order[None, :] == new_order[:, None], positions[None, :], 0), axis=1)).astype(jnp.int32)
    moved_master = jnp.take(new_master, source, axis=0)
    moved_first = jnp.take(new_a, source, axis=0)
    moved_second = jnp.take(new_b, source, axis=0)
    next_weights = moved_master.astype(jnp.bfloat16)
    combined = jnp.zeros((TOKENS, D), jnp.float32)
    for position in range(EXPERTS):
        scaling = coefficient(route_two, prob_two, new_order[position])
        combined = combined + expert_out(tokens_two, scaling, next_weights[position])
    return (moved_master, moved_first, moved_second, combined.astype(jnp.bfloat16))
```

```python
import jax
import jax.numpy as jnp
from jax import lax
from jax.experimental import pallas as pl
from jax.experimental.pallas import tpu as pltpu
from jax.sharding import Mesh
from jax.sharding import PartitionSpec as P

DP = ("dp_0", "dp_1", "dp_2")
BF = jnp.bfloat16
F32 = jnp.float32

learn_rate = 0.001
beta_one = 0.9
beta_two = 0.95
epsilon = 1e-08
decay_rate = 0.1

TILE = 256
CHUNKS = 2
VMEM_BYTES = 48 * 2**20


def from_ahead(x, axis, step):
    n = lax.axis_size(axis)
    return lax.ppermute(x, axis, [((i + step) % n, i) for i in range(n)])


def swapped(x):
    return from_ahead(x, "dp_2", 1)


def to_ahead(x, axis, step):
    return from_ahead(x, axis, -step)


def together(*values):
    return lax.optimization_barrier(values)


def rows_by(left, right):
    return lax.dot_general(
        left, right, (((1,), (1,)), ((), ())), preferred_element_type=F32
    )


def kernel_params(count=1):
    return pltpu.CompilerParams(
        dimension_semantics=("arbitrary",) * count, vmem_limit_bytes=VMEM_BYTES
    )


def whole(shape):
    return pl.BlockSpec(shape, lambda i, s: (0,) * len(shape))


def column_block(index, cols):
    return pl.ds(pl.multiple_of(index * cols, cols), cols)


def first_pass(where, tokens, cotangent, scaling, near, far):
    count, width = tokens.shape
    rows, cols = near[0].shape
    units = rows // 3
    chips = len(near)

    def body(where_ref, t, g, s_ref, *refs):
        pieces, out, held = refs[: 2 * chips], refs[-2], refs[-1]

        @pl.when(pl.program_id(0) == 0)
        def _():
            for index in range(2 * chips):
                z_half = where_ref[0] if index < chips else 1 - where_ref[0]
                block = z_half * chips + (where_ref[1] + index) % chips
                held[:, column_block(block, cols)] = pieces[index][...]

        both = rows_by(held[: 2 * units, :], t[...])
        d_act = rows_by(held[2 * units :, :], g[...]) * s_ref[...]
        gate = both[:units]
        up = both[units:]
        sig = jax.nn.sigmoid(gate)
        swish = gate * sig
        out[:units, :] = (d_act * up * sig * (1.0 + gate * (1.0 - sig))).astype(BF)
        out[units : 2 * units, :] = (d_act * swish).astype(BF)
        out[2 * units :, :] = (s_ref[...] * (swish * up)).astype(BF)

    token_block = pl.BlockSpec((TILE, width), lambda i, s: (i, 0))
    return pl.pallas_call(
        body,
        grid_spec=pltpu.PrefetchScalarGridSpec(
            num_scalar_prefetch=1,
            grid=(count // TILE,),
            in_specs=[token_block, token_block]
            + [pl.BlockSpec((1, TILE), lambda i, s: (0, i))]
            + [whole((rows, cols))] * (2 * chips),
            out_specs=pl.BlockSpec((rows, TILE), lambda i, s: (0, i)),
            scratch_shapes=[pltpu.VMEM((rows, width), BF)],
        ),
        out_shape=jax.ShapeDtypeStruct((rows, count), BF),
        compiler_params=kernel_params(),
        cost_estimate=pl.CostEstimate(
            flops=2 * count * width * rows, bytes_accessed=12 * 2**20, transcendentals=count * units
        ),
    )(where, tokens, cotangent, scaling, *near, *far)


def gradient_half(where, tokens, cotangent, factors):
    rows, count = factors[0].shape
    units = rows // 3
    chips, cols = 4, tokens[0].shape[1] // 8

    def body(where_ref, t_a, t_b, g_a, g_b, a_ref, b_ref, out):
        out[0, : 2 * units, :] = (
            jnp.dot(a_ref[: 2 * units, :], t_a[...], preferred_element_type=F32)
            + jnp.dot(b_ref[: 2 * units, :], t_b[...], preferred_element_type=F32)
        ).astype(BF)
        out[0, 2 * units :, :] = (
            jnp.dot(a_ref[2 * units :, :], g_a[...], preferred_element_type=F32)
            + jnp.dot(b_ref[2 * units :, :], g_b[...], preferred_element_type=F32)
        ).astype(BF)

    block = pl.BlockSpec((count, cols), lambda i, s: (0, s[0] * chips + (s[1] + i) % chips))
    return pl.pallas_call(
        body,
        grid_spec=pltpu.PrefetchScalarGridSpec(
            num_scalar_prefetch=1,
            grid=(chips,),
            in_specs=[block] * 4 + [whole((rows, count))] * 2,
            out_specs=pl.BlockSpec((1, rows, cols), lambda i, s: (i, 0, 0)),
        ),
        out_shape=jax.ShapeDtypeStruct((chips, rows, cols), BF),
        compiler_params=kernel_params(),
        cost_estimate=pl.CostEstimate(
            flops=4 * count * rows * chips * cols, bytes_accessed=12 * 2**20, transcendentals=0
        ),
    )(where, *tokens, *cotangent, *factors)


def second_hidden(where, tokens, scaling, own, other):
    count, width = tokens.shape
    rows, cols = own[0].shape
    units = rows // 3
    chips = len(own) // 2

    def body(where_ref, t, s_ref, *refs):
        pieces, out, held = refs[: 4 * chips], refs[-2], refs[-1]

        @pl.when(pl.program_id(0) == 0)
        def _():
            for index in range(2 * chips):
                z_half = where_ref[0] if index < chips else 1 - where_ref[0]
                span = column_block(z_half * chips + (where_ref[1] + index) % chips, cols)
                for e in range(2):
                    piece = pieces[e * 2 * chips + index]
                    for kind in range(2):
                        start = (kind * 2 + e) * units
                        held[start : start + units, span] = piece[kind * units : (kind + 1) * units, :]

        both = rows_by(t[...], held[...])
        gate = both[:, : 2 * units]
        unit = lax.broadcasted_iota(jnp.int32, (TILE, 2 * units), 1)
        scale = jnp.where(unit < units, s_ref[:, 0:1], s_ref[:, 1:2])
        out[...] = (scale * gate * jax.nn.sigmoid(gate) * both[:, 2 * units :]).astype(BF)

    return pl.pallas_call(
        body,
        grid_spec=pltpu.PrefetchScalarGridSpec(
            num_scalar_prefetch=1,
            grid=(count // TILE,),
            in_specs=[
                pl.BlockSpec((TILE, width), lambda i, s: (i, 0)),
                pl.BlockSpec((TILE, 2), lambda i, s: (i, 0)),
            ]
            + [whole((rows, cols))] * (4 * chips),
            out_specs=pl.BlockSpec((TILE, 2 * units), lambda i, s: (i, 0)),
            scratch_shapes=[pltpu.VMEM((4 * units, width), BF)],
        ),
        out_shape=jax.ShapeDtypeStruct((count, 2 * units), BF),
        compiler_params=kernel_params(),
        cost_estimate=pl.CostEstimate(
            flops=8 * count * width * units, bytes_accessed=10 * 2**20, transcendentals=2 * count * units
        ),
    )(where, tokens, scaling, *own, *other)


def second_shares(where, mixed, own, other, start, count):
    rows, cols = own[0].shape
    units = rows // 3
    chips = len(own) // 2
    slots = 4

    def body(where_ref, mix_ref, *refs):
        pieces, outs, held = refs[: 4 * chips], refs[4 * chips : 4 * chips + slots], refs[-1]
        for index in range(2 * chips):
            z_half = where_ref[0] if index < chips else 1 - where_ref[0]
            x = (where_ref[1] + index) % chips
            ahead = (z_half * 2 + x // 2 + 4 - where_ref[2]) % 4
            for core in range(2):
                place = (x % 2 * 2 + core + 4 - where_ref[3]) % 4
                span = column_block(ahead * 4 + place, cols // 2)
                lanes = slice(core * (cols // 2), (core + 1) * (cols // 2))
                for e in range(2):
                    held[e * units : (e + 1) * units, span] = pieces[e * 2 * chips + index][:, lanes]
        for ahead in range(slots):
            outs[ahead][...] = jnp.dot(
                mix_ref[...],
                held[:, ahead * 2 * cols : (ahead + 1) * 2 * cols],
                preferred_element_type=F32,
            ).astype(BF)

    mix = pl.BlockSpec((count, 2 * units), lambda i, s: (start // count, 0))
    down = pl.BlockSpec((units, cols), lambda i, s: (2, 0))
    return pl.pallas_call(
        body,
        grid_spec=pltpu.PrefetchScalarGridSpec(
            num_scalar_prefetch=1,
            grid=(1,),
            in_specs=[mix] + [down] * (4 * chips),
            out_specs=[whole((count, 2 * cols))] * slots,
            scratch_shapes=[pltpu.VMEM((2 * units, 2 * chips * cols), BF)],
        ),
        out_shape=[jax.ShapeDtypeStruct((count, 2 * cols), BF)] * slots,
        compiler_params=kernel_params(),
        cost_estimate=pl.CostEstimate(
            flops=8 * count * units * chips * cols * 2, bytes_accessed=4 * 2**20, transcendentals=0
        ),
    )(where, mixed, *own, *other)


def along_x(piece):
    return [piece] + [from_ahead(piece, "dp_1", step) for step in (1, 2, 3)]


def adamw_update(master, moment_a, moment_b, grad_sum):
    new_a = beta_one * moment_a + (1.0 - beta_one) * grad_sum
    new_b = beta_two * moment_b + (1.0 - beta_two) * grad_sum * grad_sum
    fixed_a = new_a / (1.0 - beta_one**10)
    fixed_b = new_b / (1.0 - beta_two**10)
    new_master = master - learn_rate * (
        fixed_a / (jnp.sqrt(fixed_b) + epsilon) + decay_rate * master
    )
    return (new_master, new_a, new_b)


def coefficients(routes, probs, expert_ids):
    matches = routes[:, :, None] == expert_ids[None, None, :]
    return jnp.sum(jnp.where(matches, probs[:, :, None], 0.0), axis=1)


def per_device(
    master_weights,
    first_moment,
    second_moment,
    tokens_one,
    grad_out,
    route_one,
    prob_one,
    tokens_two,
    route_two,
    prob_two,
    old_order,
    new_order,
):
    local_count, kinds, units, width = master_weights.shape
    slot = lax.axis_index("slot")
    hid = lax.axis_index("hid")
    z_half = lax.axis_index("dp_0")
    chip_x = lax.axis_index("dp_1")
    is_zero = lax.axis_index("dp_2") == 0
    where = jnp.stack([z_half, chip_x, slot, hid]).astype(jnp.int32)
    where_far = jnp.stack([1 - z_half, chip_x, slot, hid]).astype(jnp.int32)
    offset = slot * local_count
    held_ids = lax.dynamic_slice_in_dim(old_order, offset, local_count)
    ids_here = jnp.where(is_zero, held_ids, held_ids[::-1])
    rows = kinds * units

    def own_and_other(x):
        return jnp.where(is_zero, x[0], x[1]), jnp.where(is_zero, x[1], x[0])

    def in_order(mine, sibling, axis):
        return jnp.where(
            is_zero,
            jnp.concatenate([mine, sibling], axis=axis),
            jnp.concatenate([sibling, mine], axis=axis),
        )

    bf_own, bf_other = own_and_other(
        master_weights.astype(BF).reshape(local_count, rows, width)
    )
    piece, tokens_ready = together(in_order(bf_own, swapped(bf_other), 1), tokens_one)
    tokens = (tokens_one, swapped(tokens_ready))
    near = along_x(piece)
    far_piece, grad_ready, sibling_tokens = together(
        from_ahead(piece, "dp_0", 1), grad_out, tokens[1]
    )
    far = along_x(far_piece)
    tokens = (tokens_one, sibling_tokens)
    cotangent = (grad_out, swapped(grad_ready))

    states = jnp.stack([master_weights, first_moment, second_moment])
    states = states.reshape(3, local_count, rows, width)
    all_states = lax.all_gather(states, "slot")
    st_own, st_other = own_and_other(states.swapaxes(0, 1))
    pair_states = in_order(st_own, swapped(st_other), 2)

    scaling_one = coefficients(route_one, prob_one, ids_here).T
    scaling = (scaling_one[:1], swapped(scaling_one[1:]))
    factors = [
        first_pass(where, tokens[core], cotangent[core], scaling[core], near, far)
        for core in range(2)
    ]

    def chip_sum(place):
        grads = gradient_half(place, tokens, cotangent, factors)
        total = grads[0].astype(F32)
        for step in (2, 1, 3):
            total = total + to_ahead(grads[step], "dp_1", step).astype(F32)
        return total

    from_far = from_ahead(chip_sum(where_far).astype(BF), "dp_0", 1)
    pair_grads = (chip_sum(where) + from_far.astype(F32)).astype(BF)

    new_master = adamw_update(*pair_states, pair_grads.astype(F32))[0]
    next_piece = new_master.astype(BF)
    next_own = along_x(next_piece) + along_x(from_ahead(next_piece, "dp_0", 1))
    next_other = [swapped(x) for x in next_own]

    keep = jnp.where(is_zero, pair_grads[:, :width], pair_grads[:, width:])
    give = jnp.where(is_zero, pair_grads[:, width:], pair_grads[:, :width])
    all_grads = lax.all_gather(in_order(keep[None], swapped(give)[None], 0), "slot")
    positions = jnp.arange(old_order.shape[0], dtype=jnp.int32)
    source = jnp.sum(
        jnp.where(old_order[None, :] == new_order[:, None], positions[None, :], 0), axis=1
    )
    mine = lax.dynamic_slice_in_dim(source, offset, local_count)

    def moved_to(place):
        at, e = mine[place] // local_count, mine[place] % local_count
        old = lax.dynamic_slice(all_states, (at, 0, e, 0, 0), (1, 3, 1, rows, width))
        grad = lax.dynamic_slice(all_grads, (at, e, 0, 0), (1, 1, rows, width))
        return adamw_update(old[0, 0, 0], old[0, 1, 0], old[0, 2, 0], grad[0, 0].astype(F32))

    moved = [
        jnp.stack(x).reshape(master_weights.shape)
        for x in zip(*[moved_to(place) for place in range(local_count)])
    ]

    scaling_two = coefficients(route_two, prob_two, ids_here)
    mixed = second_hidden(where, tokens_two, scaling_two, next_own, next_other)
    count = tokens_two.shape[0] // CHUNKS
    shares = [
        second_shares(where, mixed, next_own, next_other, chunk * count, count)
        for chunk in range(CHUNKS)
    ]
    arrived = [
        {step: to_ahead(share[step], "slot", step) for step in (2, 1, 3)} for share in shares
    ]
    outs = []
    for chunk in range(CHUNKS):
        came = arrived[chunk]
        if chunk + 1 < CHUNKS:
            came[3], arrived[chunk + 1][2] = together(came[3], arrived[chunk + 1][2])
        else:
            came[3], moved, *outs = together(came[3], moved, *outs)
        total = shares[chunk][0].astype(F32)
        for step in (2, 1, 3):
            total = total + came[step].astype(F32)
        result = total[:, :width]
        for step in (1, 2, 3):
            part = total[:, step * width : (step + 1) * width].astype(BF)
            result = result + to_ahead(part, "hid", step).astype(F32)
        outs.append(result.astype(BF))
    return (*moved, jnp.concatenate(outs, axis=0))


def solution(mesh):
    split = Mesh(
        mesh.devices.reshape(2, 4, 2, mesh.shape["slot"], mesh.shape["hid"]),
        ("dp_0", "dp_1", "dp_2", "slot", "hid"),
    )
    states = P("slot", None, "hid", DP)
    rows = P(DP, None)
    in_specs = (states,) * 3 + (rows,) * 7 + (P(), P())
    out_specs = (states,) * 3 + (P(DP, ("slot", "hid")),)
    return jax.shard_map(
        per_device, mesh=split, in_specs=in_specs, out_specs=out_specs, check_vma=False
    )
```

```python
import jax
import jax.numpy as jnp
from jax import lax
from jax.experimental import pallas as pl
from jax.experimental.pallas import tpu as pltpu
from jax.sharding import Mesh
from jax.sharding import PartitionSpec as P

DP = ("dp_0", "dp_1", "dp_2")
BF = jnp.bfloat16
F32 = jnp.float32

learn_rate = 0.001
beta_one = 0.9
beta_two = 0.95
epsilon = 1e-08
decay_rate = 0.1

TILE = 512
CHUNKS = 2
VMEM_BYTES = 32 * 2**20


def from_ahead(x, axis, step):
    n = lax.axis_size(axis)
    return lax.ppermute(x, axis, [((i + step) % n, i) for i in range(n)])


def swapped(x):
    return from_ahead(x, "dp_2", 1)


def to_ahead(x, axis, step):
    return from_ahead(x, axis, -step)


def together(*values):
    return lax.optimization_barrier(values)


def rows_by(left, right):
    return lax.dot_general(
        left, right, (((1,), (1,)), ((), ())), preferred_element_type=F32
    )


def kernel_params(count=1):
    return pltpu.CompilerParams(
        dimension_semantics=("arbitrary",) * count, vmem_limit_bytes=VMEM_BYTES
    )


def whole(shape):
    return pl.BlockSpec(shape, lambda i, s: (0,) * len(shape))


def column_block(index, cols):
    return pl.ds(pl.multiple_of(index * cols, cols), cols)


def first_half(where, far, tokens, scaled_grad, weights, partial=None):
    count, width = tokens.shape
    chips, rows, cols = weights.shape
    units = rows // 3
    last = partial is not None

    def body(where_ref, t, g, pieces, *refs):
        out, held = refs[-2:]

        @pl.when(pl.program_id(0) == 0)
        def _():
            for step in range(chips):
                held[:, column_block((where_ref[1] + step) % chips, cols)] = pieces[step]

        both = rows_by(held[: 2 * units, :], t[...])
        d_act = rows_by(held[2 * units :, :], g[...])
        if not last:
            out[: 2 * units, :] = both
            out[2 * units :, :] = d_act
            return
        gate = both[:units] + refs[0][:units, :]
        up = both[units:] + refs[0][units : 2 * units, :]
        d_act = d_act + refs[0][2 * units :, :]
        sig = jax.nn.sigmoid(gate)
        swish = gate * sig
        out[:units, :] = (d_act * up * sig * (1.0 + gate * (1.0 - sig))).astype(BF)
        out[units : 2 * units, :] = (d_act * swish).astype(BF)
        out[2 * units :, :] = (swish * up).astype(BF)

    token_block = pl.BlockSpec((TILE, width // 2), lambda i, s: (i, 1 - s[0] if far else s[0]))
    by_token = pl.BlockSpec((rows, TILE), lambda i, s: (0, i))
    return pl.pallas_call(
        body,
        grid_spec=pltpu.PrefetchScalarGridSpec(
            num_scalar_prefetch=1,
            grid=(count // TILE,),
            in_specs=[token_block, token_block, whole(weights.shape)] + [by_token] * last,
            out_specs=by_token,
            scratch_shapes=[pltpu.VMEM((rows, width // 2), BF)],
        ),
        out_shape=jax.ShapeDtypeStruct((rows, count), BF if last else F32),
        compiler_params=kernel_params(),
        cost_estimate=pl.CostEstimate(
            flops=count * width * rows, bytes_accessed=8 * 2**20, transcendentals=last * count * units
        ),
    )(where, tokens, scaled_grad, weights, *([partial] if last else []))


def gradient_half(where, tokens, cotangent, factors):
    rows, count = factors[0].shape
    units = rows // 3
    chips, cols = 4, tokens[0].shape[1] // 8

    def body(where_ref, t_a, t_b, g_a, g_b, a_ref, b_ref, out):
        out[0, : 2 * units, :] = (
            jnp.dot(a_ref[: 2 * units, :], t_a[...], preferred_element_type=F32)
            + jnp.dot(b_ref[: 2 * units, :], t_b[...], preferred_element_type=F32)
        ).astype(BF)
        out[0, 2 * units :, :] = (
            jnp.dot(a_ref[2 * units :, :], g_a[...], preferred_element_type=F32)
            + jnp.dot(b_ref[2 * units :, :], g_b[...], preferred_element_type=F32)
        ).astype(BF)

    block = pl.BlockSpec((count, cols), lambda i, s: (0, s[0] * chips + (s[1] + i) % chips))
    return pl.pallas_call(
        body,
        grid_spec=pltpu.PrefetchScalarGridSpec(
            num_scalar_prefetch=1,
            grid=(chips,),
            in_specs=[block] * 4 + [whole((rows, count))] * 2,
            out_specs=pl.BlockSpec((1, rows, cols), lambda i, s: (i, 0, 0)),
        ),
        out_shape=jax.ShapeDtypeStruct((chips, rows, cols), BF),
        compiler_params=kernel_params(),
        cost_estimate=pl.CostEstimate(
            flops=4 * count * rows * chips * cols, bytes_accessed=12 * 2**20, transcendentals=0
        ),
    )(where, *tokens, *cotangent, *factors)


def down_blocks(where_ref, chips):
    for half in range(2):
        for step in range(chips):
            z_half = 1 - where_ref[0] if half else where_ref[0]
            x = (where_ref[1] + step) % chips
            ahead = (z_half * 2 + x // 2 + 4 - where_ref[2]) % 4
            for core in range(2):
                yield half, step, core, ahead, (x % 2 * 2 + core + 4 - where_ref[3]) % 4


def held_up(where_ref, pieces, held):
    chips, rows, cols = pieces[0].shape
    units = rows // 3
    for step in range(chips):
        span = column_block((where_ref[1] + step) % chips, cols)
        for e in range(2):
            for kind in range(2):
                start = (kind * 2 + e) * units
                held[start : start + units, span] = pieces[e][step, kind * units : (kind + 1) * units, :]


def second_near(where, tokens, own, other):
    count, width = tokens.shape
    chips, rows, cols = own.shape
    units = rows // 3

    def body(where_ref, t, own_ref, oth_ref, out, held):
        @pl.when(pl.program_id(0) == 0)
        def _():
            held_up(where_ref, (own_ref, oth_ref), held)

        out[...] = rows_by(t[...], held[...])

    return pl.pallas_call(
        body,
        grid_spec=pltpu.PrefetchScalarGridSpec(
            num_scalar_prefetch=1,
            grid=(count // TILE,),
            in_specs=[pl.BlockSpec((TILE, width // 2), lambda i, s: (i, s[0]))]
            + [whole(own.shape)] * 2,
            out_specs=pl.BlockSpec((TILE, 4 * units), lambda i, s: (i, 0)),
            scratch_shapes=[pltpu.VMEM((4 * units, width // 2), BF)],
        ),
        out_shape=jax.ShapeDtypeStruct((count, 4 * units), F32),
        compiler_params=kernel_params(),
        cost_estimate=pl.CostEstimate(
            flops=4 * count * width * units, bytes_accessed=8 * 2**20, transcendentals=0
        ),
    )(where, tokens, own, other)


def second_hidden(where, tokens, scaling, partial, weights):
    count, width = tokens.shape
    chips, rows, cols = weights[0].shape
    units = rows // 3
    lanes = cols // 2

    def body(where_ref, t, s_ref, part, own_n, oth_n, own_f, oth_f, mix_out, share_out, held, down):
        @pl.when(pl.program_id(0) == 0)
        def _():
            held_up(where_ref, (own_f, oth_f), held)
            pieces = ((own_n, oth_n), (own_f, oth_f))
            for half, step, core, ahead, place in down_blocks(where_ref, chips):

                @pl.when(ahead == 2)
                def _():
                    first = 2 * units if half else 0
                    for e in range(2):
                        down[e * units : (e + 1) * units, column_block(place, lanes)] = pieces[half][e][
                            step, first : first + units, core * lanes : (core + 1) * lanes
                        ]

        both = rows_by(t[...], held[...]) + part[...]
        gate = both[:, : 2 * units]
        unit = lax.broadcasted_iota(jnp.int32, (TILE, 2 * units), 1)
        scale = jnp.where(unit < units, s_ref[:, 0:1], s_ref[:, 1:2])
        mixed = (scale * gate * jax.nn.sigmoid(gate) * both[:, 2 * units :]).astype(BF)
        mix_out[...] = mixed
        share_out[...] = jnp.dot(mixed, down[...], preferred_element_type=F32).astype(BF)

    def by_token(size):
        return pl.BlockSpec((TILE, size), lambda i, s: (i, 0))

    return pl.pallas_call(
        body,
        grid_spec=pltpu.PrefetchScalarGridSpec(
            num_scalar_prefetch=1,
            grid=(count // TILE,),
            in_specs=[pl.BlockSpec((TILE, width // 2), lambda i, s: (i, 1 - s[0]))]
            + [by_token(2), by_token(4 * units)]
            + [pl.BlockSpec((chips, units, cols), lambda i, s: (0, 2, 0))] * 2
            + [whole(weights[0].shape)] * 2,
            out_specs=[by_token(2 * units), by_token(4 * lanes)],
            scratch_shapes=[
                pltpu.VMEM((4 * units, width // 2), BF),
                pltpu.VMEM((2 * units, 4 * lanes), BF),
            ],
        ),
        out_shape=[
            jax.ShapeDtypeStruct((count, 2 * units), BF),
            jax.ShapeDtypeStruct((count, 4 * lanes), BF),
        ],
        compiler_params=kernel_params(),
        cost_estimate=pl.CostEstimate(
            flops=5 * count * width * units, bytes_accessed=10 * 2**20, transcendentals=2 * count * units
        ),
    )(where, tokens, scaling, partial, *weights)


def second_shares(where, mixed, weights, parts):
    count = mixed.shape[0] // parts
    chips, rows, cols = weights[0].shape
    units = rows // 3
    lanes = cols // 2
    steps = (1, 3, 0)

    def body(where_ref, mix_ref, own_n, oth_n, own_f, oth_f, *refs):
        outs, held = refs[:-1], refs[-1]
        pieces = ((own_n, oth_n), (own_f, oth_f))
        for half, step, core, ahead, place in down_blocks(where_ref, chips):
            for e in range(2):
                held[e * units : (e + 1) * units, column_block(ahead * 4 + place, lanes)] = pieces[half][e][
                    step, :, core * lanes : (core + 1) * lanes
                ]
        for part in range(parts):
            for place, step in enumerate(steps):
                outs[part * len(steps) + place][...] = jnp.dot(
                    mix_ref[part * count : (part + 1) * count, :],
                    held[:, step * 4 * lanes : (step + 1) * 4 * lanes],
                    preferred_element_type=F32,
                ).astype(BF)

    down = pl.BlockSpec((chips, units, cols), lambda i, s: (0, 2, 0))
    shares = pl.pallas_call(
        body,
        grid_spec=pltpu.PrefetchScalarGridSpec(
            num_scalar_prefetch=1,
            grid=(1,),
            in_specs=[whole(mixed.shape)] + [down] * 4,
            out_specs=[whole((count, 2 * cols))] * (len(steps) * parts),
            scratch_shapes=[pltpu.VMEM((2 * units, 2 * chips * cols), BF)],
        ),
        out_shape=[jax.ShapeDtypeStruct((count, 2 * cols), BF)] * (len(steps) * parts),
        compiler_params=kernel_params(),
        cost_estimate=pl.CostEstimate(
            flops=6 * count * parts * units * chips * cols * 2, bytes_accessed=6 * 2**20, transcendentals=0
        ),
    )(where, mixed, *weights)
    return [
        dict(zip(steps, shares[part * len(steps) : (part + 1) * len(steps)])) for part in range(parts)
    ]


def along_x(piece):
    return [piece] + [from_ahead(piece, "dp_1", step) for step in (1, 2, 3)]


def adamw_update(master, moment_a, moment_b, grad_sum):
    new_a = beta_one * moment_a + (1.0 - beta_one) * grad_sum
    new_b = beta_two * moment_b + (1.0 - beta_two) * grad_sum * grad_sum
    fixed_a = new_a / (1.0 - beta_one**10)
    fixed_b = new_b / (1.0 - beta_two**10)
    new_master = master - learn_rate * (
        fixed_a / (jnp.sqrt(fixed_b) + epsilon) + decay_rate * master
    )
    return (new_master, new_a, new_b)


def moved_states(mine, states, grads):
    _, kinds, local, rows, width = states.shape

    def body(mine_ref, old, grad, *outs):
        new = adamw_update(old[0, 0, 0], old[0, 1, 0], old[0, 2, 0], grad[0, 0].astype(F32))
        for value, out in zip(new, outs):
            out[0] = value

    return pl.pallas_call(
        body,
        grid_spec=pltpu.PrefetchScalarGridSpec(
            num_scalar_prefetch=1,
            grid=(local,),
            in_specs=[
                pl.BlockSpec((1, kinds, 1, rows, width), lambda i, s: (s[i] // local, 0, s[i] % local, 0, 0)),
                pl.BlockSpec((1, 1, rows, width), lambda i, s: (s[i] // local, s[i] % local, 0, 0)),
            ],
            out_specs=[pl.BlockSpec((1, rows, width), lambda i, s: (i, 0, 0))] * kinds,
        ),
        out_shape=[jax.ShapeDtypeStruct((local, rows, width), F32)] * kinds,
        compiler_params=kernel_params(),
        cost_estimate=pl.CostEstimate(
            flops=40 * local * rows * width, bytes_accessed=4 * 2**20, transcendentals=2 * local * rows * width
        ),
    )(mine, states, grads)


def coefficients(routes, probs, expert_ids):
    matches = routes[:, :, None] == expert_ids[None, None, :]
    return jnp.sum(jnp.where(matches, probs[:, :, None], 0.0), axis=1)


def per_device(
    master_weights,
    first_moment,
    second_moment,
    tokens_one,
    grad_out,
    route_one,
    prob_one,
    tokens_two,
    route_two,
    prob_two,
    old_order,
    new_order,
):
    local_count, kinds, units, width = master_weights.shape
    slot = lax.axis_index("slot")
    hid = lax.axis_index("hid")
    z_half = lax.axis_index("dp_0")
    chip_x = lax.axis_index("dp_1")
    is_zero = lax.axis_index("dp_2") == 0
    where = jnp.stack([z_half, chip_x, slot, hid]).astype(jnp.int32)
    where_far = jnp.stack([1 - z_half, chip_x, slot, hid]).astype(jnp.int32)
    offset = slot * local_count
    held_ids = lax.dynamic_slice_in_dim(old_order, offset, local_count)
    ids_here = jnp.where(is_zero, held_ids, held_ids[::-1])
    rows = kinds * units

    def own_and_other(x):
        return jnp.where(is_zero, x[0], x[1]), jnp.where(is_zero, x[1], x[0])

    def in_order(mine, sibling, axis):
        return jnp.where(
            is_zero,
            jnp.concatenate([mine, sibling], axis=axis),
            jnp.concatenate([sibling, mine], axis=axis),
        )

    bf_own, bf_other = own_and_other(
        master_weights.astype(BF).reshape(local_count, rows, width)
    )
    scaling_one = coefficients(route_one, prob_one, ids_here)
    scaled_own, scaled_other = [
        (scaling_one[:, e : e + 1] * grad_out.astype(F32)).astype(BF) for e in range(2)
    ]
    piece, tokens_ready = together(in_order(bf_own, swapped(bf_other), 1), tokens_one)
    far_piece, near, sibling_tokens, scaled_other = together(
        from_ahead(piece, "dp_0", 1), along_x(piece), swapped(tokens_ready), scaled_other
    )
    tokens = (tokens_one, sibling_tokens)
    cotangent = (scaled_own, swapped(scaled_other))

    states = jnp.stack([master_weights, first_moment, second_moment])
    states = states.reshape(3, local_count, rows, width)
    all_states = lax.all_gather(states, "slot")
    st_own, st_other = own_and_other(states.swapaxes(0, 1))
    pair_states = in_order(st_own, swapped(st_other), 2)

    near = jnp.stack(near)
    far, partials = together(
        along_x(far_piece),
        [first_half(where, False, tokens[core], cotangent[core], near) for core in range(2)],
    )
    far = jnp.stack(far)
    factors = [
        first_half(where, True, tokens[core], cotangent[core], far, partials[core])
        for core in range(2)
    ]

    def chip_sum(place):
        grads = gradient_half(place, tokens, cotangent, factors)
        total = grads[0].astype(F32)
        for step in (2, 1, 3):
            total = total + to_ahead(grads[step], "dp_1", step).astype(F32)
        return total

    from_far = from_ahead(chip_sum(where_far).astype(BF), "dp_0", 1)
    pair_grads = (chip_sum(where) + from_far.astype(F32)).astype(BF)

    new_master = adamw_update(*pair_states, pair_grads.astype(F32))[0]
    next_piece = new_master.astype(BF)
    keep = jnp.where(is_zero, pair_grads[:, :width], pair_grads[:, width:])
    give = jnp.where(is_zero, pair_grads[:, width:], pair_grads[:, :width])
    next_far, next_near, grads = together(
        from_ahead(next_piece, "dp_0", 1),
        along_x(next_piece),
        in_order(keep[None], swapped(give)[None], 0),
    )
    all_grads = lax.all_gather(grads, "slot")
    next_near = jnp.stack(next_near)
    other_near = swapped(next_near)
    next_far, partial, all_grads = together(
        along_x(next_far), second_near(where, tokens_two, next_near, other_near), all_grads
    )
    next_far = jnp.stack(next_far)
    next_weights = (next_near, other_near, next_far, swapped(next_far))

    positions = jnp.arange(old_order.shape[0], dtype=jnp.int32)
    source = jnp.sum(
        jnp.where(old_order[None, :] == new_order[:, None], positions[None, :], 0), axis=1
    )
    mine = lax.dynamic_slice_in_dim(source, offset, local_count)

    scaling_two = coefficients(route_two, prob_two, ids_here)
    mixed, opposite = second_hidden(where, tokens_two, scaling_two, partial, next_weights)
    from_opposite = to_ahead(opposite, "slot", 2)
    mine, opposite = together(mine, opposite)
    moved = [
        x.reshape(master_weights.shape) for x in moved_states(mine, all_states, all_grads)
    ]
    shares = second_shares(where, mixed, next_weights, CHUNKS)
    count = tokens_two.shape[0] // CHUNKS
    outs = []
    for chunk, share in enumerate(shares):
        came = [to_ahead(share[step], "slot", step) for step in (1, 3)]
        if chunk == 0:
            came, moved = together(came, moved)
        else:
            came, outs = together(came, outs)
        total = share[0].astype(F32)
        for value in (from_opposite[chunk * count : (chunk + 1) * count], *came):
            total = total + value.astype(F32)
        result = total[:, :width]
        for step in (1, 2, 3):
            part = total[:, step * width : (step + 1) * width].astype(BF)
            result = result + to_ahead(part, "hid", step).astype(F32)
        outs.append(result.astype(BF))
    return (*moved, jnp.concatenate(outs, axis=0))


def solution(mesh):
    split = Mesh(
        mesh.devices.reshape(2, 4, 2, mesh.shape["slot"], mesh.shape["hid"]),
        ("dp_0", "dp_1", "dp_2", "slot", "hid"),
    )
    states = P("slot", None, "hid", DP)
    rows = P(DP, None)
    in_specs = (states,) * 3 + (rows,) * 7 + (P(), P())
    out_specs = (states,) * 3 + (P(DP, ("slot", "hid")),)
    return jax.shard_map(
        per_device, mesh=split, in_specs=in_specs, out_specs=out_specs, check_vma=False
    )
```

```python
import jax
import jax.numpy as jnp
from jax import lax
from jax.experimental import pallas as pl
from jax.experimental.pallas import tpu as pltpu
from jax.sharding import Mesh
from jax.sharding import PartitionSpec as P

DP = ("dp_0", "dp_1", "dp_2")
BF = jnp.bfloat16
F32 = jnp.float32

learn_rate = 0.001
beta_one = 0.9
beta_two = 0.95
epsilon = 1e-08
decay_rate = 0.1

TILE = 512
CHUNKS = 2
VMEM_BYTES = 32 * 2**20


def from_ahead(x, axis, step):
    n = lax.axis_size(axis)
    return lax.ppermute(x, axis, [((i + step) % n, i) for i in range(n)])


def swapped(x):
    return from_ahead(x, "dp_2", 1)


def to_ahead(x, axis, step):
    return from_ahead(x, axis, -step)


def together(*values):
    return lax.optimization_barrier(values)


def rows_by(left, right):
    return lax.dot_general(
        left, right, (((1,), (1,)), ((), ())), preferred_element_type=F32
    )


def kernel_params(count=1):
    return pltpu.CompilerParams(
        dimension_semantics=("arbitrary",) * count, vmem_limit_bytes=VMEM_BYTES
    )


def whole(shape):
    return pl.BlockSpec(shape, lambda i, s: (0,) * len(shape))


def column_block(index, cols):
    return pl.ds(pl.multiple_of(index * cols, cols), cols)


def first_half(where, far, tokens, scaled_grad, weights, partial=None):
    count, width = tokens.shape
    chips, rows, cols = weights.shape
    units = rows // 3
    last = partial is not None

    def body(where_ref, t, g, pieces, *refs):
        out, held = refs[-2:]

        @pl.when(pl.program_id(0) == 0)
        def _():
            for step in range(chips):
                held[:, column_block((where_ref[1] + step) % chips, cols)] = pieces[step]

        both = rows_by(held[: 2 * units, :], t[...])
        d_act = rows_by(held[2 * units :, :], g[...])
        if not last:
            out[: 2 * units, :] = both
            out[2 * units :, :] = d_act
            return
        gate = both[:units] + refs[0][:units, :]
        up = both[units:] + refs[0][units : 2 * units, :]
        d_act = d_act + refs[0][2 * units :, :]
        sig = jax.nn.sigmoid(gate)
        swish = gate * sig
        out[:units, :] = (d_act * up * sig * (1.0 + gate * (1.0 - sig))).astype(BF)
        out[units : 2 * units, :] = (d_act * swish).astype(BF)
        out[2 * units :, :] = (swish * up).astype(BF)

    token_block = pl.BlockSpec((TILE, width // 2), lambda i, s: (i, 1 - s[0] if far else s[0]))
    by_token = pl.BlockSpec((rows, TILE), lambda i, s: (0, i))
    return pl.pallas_call(
        body,
        grid_spec=pltpu.PrefetchScalarGridSpec(
            num_scalar_prefetch=1,
            grid=(count // TILE,),
            in_specs=[token_block, token_block, whole(weights.shape)] + [by_token] * last,
            out_specs=by_token,
            scratch_shapes=[pltpu.VMEM((rows, width // 2), BF)],
        ),
        out_shape=jax.ShapeDtypeStruct((rows, count), BF if last else F32),
        compiler_params=kernel_params(),
        cost_estimate=pl.CostEstimate(
            flops=count * width * rows, bytes_accessed=8 * 2**20, transcendentals=last * count * units
        ),
    )(where, tokens, scaled_grad, weights, *([partial] if last else []))


def gradient_half(where, tokens, cotangent, factors):
    rows, count = factors[0].shape
    units = rows // 3
    chips, cols = 4, tokens[0].shape[1] // 8

    def body(where_ref, t_a, t_b, g_a, g_b, a_ref, b_ref, out):
        out[0, : 2 * units, :] = (
            jnp.dot(a_ref[: 2 * units, :], t_a[...], preferred_element_type=F32)
            + jnp.dot(b_ref[: 2 * units, :], t_b[...], preferred_element_type=F32)
        ).astype(BF)
        out[0, 2 * units :, :] = (
            jnp.dot(a_ref[2 * units :, :], g_a[...], preferred_element_type=F32)
            + jnp.dot(b_ref[2 * units :, :], g_b[...], preferred_element_type=F32)
        ).astype(BF)

    block = pl.BlockSpec((count, cols), lambda i, s: (0, s[0] * chips + (s[1] + i) % chips))
    return pl.pallas_call(
        body,
        grid_spec=pltpu.PrefetchScalarGridSpec(
            num_scalar_prefetch=1,
            grid=(chips,),
            in_specs=[block] * 4 + [whole((rows, count))] * 2,
            out_specs=pl.BlockSpec((1, rows, cols), lambda i, s: (i, 0, 0)),
        ),
        out_shape=jax.ShapeDtypeStruct((chips, rows, cols), BF),
        compiler_params=kernel_params(),
        cost_estimate=pl.CostEstimate(
            flops=4 * count * rows * chips * cols, bytes_accessed=12 * 2**20, transcendentals=0
        ),
    )(where, *tokens, *cotangent, *factors)


def down_blocks(where_ref, chips):
    for half in range(2):
        for step in range(chips):
            z_half = 1 - where_ref[0] if half else where_ref[0]
            x = (where_ref[1] + step) % chips
            ahead = (z_half * 2 + x // 2 + 4 - where_ref[2]) % 4
            for core in range(2):
                yield half, step, core, ahead, (x % 2 * 2 + core + 4 - where_ref[3]) % 4


def held_up(where_ref, pieces, held):
    chips, rows, cols = pieces[0].shape
    units = rows // 3
    for step in range(chips):
        span = column_block((where_ref[1] + step) % chips, cols)
        for e in range(2):
            for kind in range(2):
                start = (kind * 2 + e) * units
                held[start : start + units, span] = pieces[e][step, kind * units : (kind + 1) * units, :]


def second_near(where, tokens, own, other):
    count, width = tokens.shape
    chips, rows, cols = own.shape
    units = rows // 3

    def body(where_ref, t, own_ref, oth_ref, out, held):
        @pl.when(pl.program_id(0) == 0)
        def _():
            held_up(where_ref, (own_ref, oth_ref), held)

        out[...] = rows_by(t[...], held[...])

    return pl.pallas_call(
        body,
        grid_spec=pltpu.PrefetchScalarGridSpec(
            num_scalar_prefetch=1,
            grid=(count // TILE,),
            in_specs=[pl.BlockSpec((TILE, width // 2), lambda i, s: (i, s[0]))]
            + [whole(own.shape)] * 2,
            out_specs=pl.BlockSpec((TILE, 4 * units), lambda i, s: (i, 0)),
            scratch_shapes=[pltpu.VMEM((4 * units, width // 2), BF)],
        ),
        out_shape=jax.ShapeDtypeStruct((count, 4 * units), F32),
        compiler_params=kernel_params(),
        cost_estimate=pl.CostEstimate(
            flops=4 * count * width * units, bytes_accessed=8 * 2**20, transcendentals=0
        ),
    )(where, tokens, own, other)


def second_hidden(where, tokens, scaling, partial, weights):
    count, width = tokens.shape
    chips, rows, cols = weights[0].shape
    units = rows // 3
    lanes = cols // 2

    def body(where_ref, t, s_ref, part, own_n, oth_n, own_f, oth_f, mix_out, share_out, held, down):
        @pl.when(pl.program_id(0) == 0)
        def _():
            held_up(where_ref, (own_f, oth_f), held)
            pieces = ((own_n, oth_n), (own_f, oth_f))
            for half, step, core, ahead, place in down_blocks(where_ref, chips):

                @pl.when(ahead == 2)
                def _():
                    first = 2 * units if half else 0
                    for e in range(2):
                        down[e * units : (e + 1) * units, column_block(place, lanes)] = pieces[half][e][
                            step, first : first + units, core * lanes : (core + 1) * lanes
                        ]

        both = rows_by(t[...], held[...]) + part[...]
        gate = both[:, : 2 * units]
        unit = lax.broadcasted_iota(jnp.int32, (TILE, 2 * units), 1)
        scale = jnp.where(unit < units, s_ref[:, 0:1], s_ref[:, 1:2])
        mixed = (scale * gate * jax.nn.sigmoid(gate) * both[:, 2 * units :]).astype(BF)
        mix_out[...] = mixed
        share_out[...] = jnp.dot(mixed, down[...], preferred_element_type=F32).astype(BF)

    def by_token(size):
        return pl.BlockSpec((TILE, size), lambda i, s: (i, 0))

    return pl.pallas_call(
        body,
        grid_spec=pltpu.PrefetchScalarGridSpec(
            num_scalar_prefetch=1,
            grid=(count // TILE,),
            in_specs=[pl.BlockSpec((TILE, width // 2), lambda i, s: (i, 1 - s[0]))]
            + [by_token(2), by_token(4 * units)]
            + [pl.BlockSpec((chips, units, cols), lambda i, s: (0, 2, 0))] * 2
            + [whole(weights[0].shape)] * 2,
            out_specs=[by_token(2 * units), by_token(4 * lanes)],
            scratch_shapes=[
                pltpu.VMEM((4 * units, width // 2), BF),
                pltpu.VMEM((2 * units, 4 * lanes), BF),
            ],
        ),
        out_shape=[
            jax.ShapeDtypeStruct((count, 2 * units), BF),
            jax.ShapeDtypeStruct((count, 4 * lanes), BF),
        ],
        compiler_params=kernel_params(),
        cost_estimate=pl.CostEstimate(
            flops=5 * count * width * units, bytes_accessed=10 * 2**20, transcendentals=2 * count * units
        ),
    )(where, tokens, scaling, partial, *weights)


def second_shares(where, mixed, weights, parts):
    count = mixed.shape[0] // parts
    chips, rows, cols = weights[0].shape
    units = rows // 3
    lanes = cols // 2
    steps = (1, 3, 0)

    def body(where_ref, mix_ref, own_n, oth_n, own_f, oth_f, *refs):
        outs, held = refs[:-1], refs[-1]
        pieces = ((own_n, oth_n), (own_f, oth_f))
        for half, step, core, ahead, place in down_blocks(where_ref, chips):
            for e in range(2):
                held[e * units : (e + 1) * units, column_block(ahead * 4 + place, lanes)] = pieces[half][e][
                    step, :, core * lanes : (core + 1) * lanes
                ]
        for part in range(parts):
            for place, step in enumerate(steps):
                outs[part * len(steps) + place][...] = jnp.dot(
                    mix_ref[part * count : (part + 1) * count, :],
                    held[:, step * 4 * lanes : (step + 1) * 4 * lanes],
                    preferred_element_type=F32,
                ).astype(BF)

    down = pl.BlockSpec((chips, units, cols), lambda i, s: (0, 2, 0))
    shares = pl.pallas_call(
        body,
        grid_spec=pltpu.PrefetchScalarGridSpec(
            num_scalar_prefetch=1,
            grid=(1,),
            in_specs=[whole(mixed.shape)] + [down] * 4,
            out_specs=[whole((count, 2 * cols))] * (len(steps) * parts),
            scratch_shapes=[pltpu.VMEM((2 * units, 2 * chips * cols), BF)],
        ),
        out_shape=[jax.ShapeDtypeStruct((count, 2 * cols), BF)] * (len(steps) * parts),
        compiler_params=kernel_params(),
        cost_estimate=pl.CostEstimate(
            flops=6 * count * parts * units * chips * cols * 2, bytes_accessed=6 * 2**20, transcendentals=0
        ),
    )(where, mixed, *weights)
    return [
        dict(zip(steps, shares[part * len(steps) : (part + 1) * len(steps)])) for part in range(parts)
    ]


def along_x(piece):
    return [piece] + [from_ahead(piece, "dp_1", step) for step in (1, 2, 3)]


def adamw_update(master, moment_a, moment_b, grad_sum):
    new_a = beta_one * moment_a + (1.0 - beta_one) * grad_sum
    new_b = beta_two * moment_b + (1.0 - beta_two) * grad_sum * grad_sum
    fixed_a = new_a / (1.0 - beta_one**10)
    fixed_b = new_b / (1.0 - beta_two**10)
    new_master = master - learn_rate * (
        fixed_a / (jnp.sqrt(fixed_b) + epsilon) + decay_rate * master
    )
    return (new_master, new_a, new_b)


def moved_states(mine, states, grads):
    _, kinds, local, rows, width = states.shape

    def body(mine_ref, old, grad, *outs):
        new = adamw_update(old[0, 0, 0], old[0, 1, 0], old[0, 2, 0], grad[0, 0].astype(F32))
        for value, out in zip(new, outs):
            out[0] = value

    return pl.pallas_call(
        body,
        grid_spec=pltpu.PrefetchScalarGridSpec(
            num_scalar_prefetch=1,
            grid=(local,),
            in_specs=[
                pl.BlockSpec((1, kinds, 1, rows, width), lambda i, s: (s[i] // local, 0, s[i] % local, 0, 0)),
                pl.BlockSpec((1, 1, rows, width), lambda i, s: (s[i] // local, s[i] % local, 0, 0)),
            ],
            out_specs=[pl.BlockSpec((1, rows, width), lambda i, s: (i, 0, 0))] * kinds,
        ),
        out_shape=[jax.ShapeDtypeStruct((local, rows, width), F32)] * kinds,
        compiler_params=kernel_params(),
        cost_estimate=pl.CostEstimate(
            flops=40 * local * rows * width, bytes_accessed=4 * 2**20, transcendentals=2 * local * rows * width
        ),
    )(mine, states, grads)


def coefficients(routes, probs, expert_ids):
    matches = routes[:, :, None] == expert_ids[None, None, :]
    return jnp.sum(jnp.where(matches, probs[:, :, None], 0.0), axis=1)


def per_device(
    master_weights,
    first_moment,
    second_moment,
    tokens_one,
    grad_out,
    route_one,
    prob_one,
    tokens_two,
    route_two,
    prob_two,
    old_order,
    new_order,
):
    local_count, kinds, units, width = master_weights.shape
    slot = lax.axis_index("slot")
    hid = lax.axis_index("hid")
    z_half = lax.axis_index("dp_0")
    chip_x = lax.axis_index("dp_1")
    is_zero = lax.axis_index("dp_2") == 0
    where = jnp.stack([z_half, chip_x, slot, hid]).astype(jnp.int32)
    where_far = jnp.stack([1 - z_half, chip_x, slot, hid]).astype(jnp.int32)
    offset = slot * local_count
    held_ids = lax.dynamic_slice_in_dim(old_order, offset, local_count)
    ids_here = jnp.where(is_zero, held_ids, held_ids[::-1])
    rows = kinds * units

    def own_and_other(x):
        return jnp.where(is_zero, x[0], x[1]), jnp.where(is_zero, x[1], x[0])

    def in_order(mine, sibling, axis):
        return jnp.where(
            is_zero,
            jnp.concatenate([mine, sibling], axis=axis),
            jnp.concatenate([sibling, mine], axis=axis),
        )

    bf_own, bf_other = own_and_other(
        master_weights.astype(BF).reshape(local_count, rows, width)
    )
    scaling_one = coefficients(route_one, prob_one, ids_here)
    scaled_own, scaled_other = [
        (scaling_one[:, e : e + 1] * grad_out.astype(F32)).astype(BF) for e in range(2)
    ]
    piece, tokens_ready = together(in_order(bf_own, swapped(bf_other), 1), tokens_one)
    far_piece, near, sibling_tokens, scaled_other = together(
        from_ahead(piece, "dp_0", 1), along_x(piece), swapped(tokens_ready), scaled_other
    )
    tokens = (tokens_one, sibling_tokens)
    cotangent = (scaled_own, swapped(scaled_other))

    states = jnp.stack([master_weights, first_moment, second_moment])
    states = states.reshape(3, local_count, rows, width)
    all_states = lax.all_gather(states, "slot")
    st_own, st_other = own_and_other(states.swapaxes(0, 1))
    pair_states = in_order(st_own, swapped(st_other), 2)

    near = jnp.stack(near)
    far, partials = together(
        along_x(far_piece),
        [first_half(where, False, tokens[core], cotangent[core], near) for core in range(2)],
    )
    far = jnp.stack(far)
    factors = [
        first_half(where, True, tokens[core], cotangent[core], far, partials[core])
        for core in range(2)
    ]

    def chip_sum(place):
        grads = gradient_half(place, tokens, cotangent, factors)
        total = grads[0].astype(F32)
        for step in (2, 1, 3):
            total = total + to_ahead(grads[step], "dp_1", step).astype(F32)
        return total

    from_far = from_ahead(chip_sum(where_far).astype(BF), "dp_0", 1)
    pair_grads = (chip_sum(where) + from_far.astype(F32)).astype(BF)

    new_master = adamw_update(*pair_states, pair_grads.astype(F32))[0]
    next_piece = new_master.astype(BF)
    keep = jnp.where(is_zero, pair_grads[:, :width], pair_grads[:, width:])
    give = jnp.where(is_zero, pair_grads[:, width:], pair_grads[:, :width])
    next_far, next_near, grads = together(
        from_ahead(next_piece, "dp_0", 1),
        along_x(next_piece),
        in_order(keep[None], swapped(give)[None], 0),
    )
    grads, all_states = together(grads, all_states)
    all_grads = lax.all_gather(grads, "slot")
    next_near = jnp.stack(next_near)
    other_near = swapped(next_near)
    next_far, partial = together(
        along_x(next_far), second_near(where, tokens_two, next_near, other_near)
    )
    next_far = jnp.stack(next_far)
    other_far, all_grads = together(swapped(next_far), all_grads)
    next_weights = (next_near, other_near, next_far, other_far)

    positions = jnp.arange(old_order.shape[0], dtype=jnp.int32)
    source = jnp.sum(
        jnp.where(old_order[None, :] == new_order[:, None], positions[None, :], 0), axis=1
    )
    mine = lax.dynamic_slice_in_dim(source, offset, local_count)

    scaling_two = coefficients(route_two, prob_two, ids_here)
    mixed, opposite = second_hidden(where, tokens_two, scaling_two, partial, next_weights)
    from_opposite = to_ahead(opposite, "slot", 2)
    mine, opposite = together(mine, opposite)
    moved = [
        x.reshape(master_weights.shape) for x in moved_states(mine, all_states, all_grads)
    ]
    shares = second_shares(where, mixed, next_weights, CHUNKS)
    count = tokens_two.shape[0] // CHUNKS
    outs = []
    for chunk, share in enumerate(shares):
        came = [to_ahead(share[step], "slot", step) for step in (1, 3)]
        if chunk == 0:
            came, moved = together(came, moved)
        else:
            came, outs = together(came, outs)
        total = share[0].astype(F32)
        for value in (from_opposite[chunk * count : (chunk + 1) * count], *came):
            total = total + value.astype(F32)
        result = total[:, :width]
        for step in (1, 2, 3):
            part = total[:, step * width : (step + 1) * width].astype(BF)
            result = result + to_ahead(part, "hid", step).astype(F32)
        outs.append(result.astype(BF))
    return (*moved, jnp.concatenate(outs, axis=0))


def solution(mesh):
    split = Mesh(
        mesh.devices.reshape(2, 4, 2, mesh.shape["slot"], mesh.shape["hid"]),
        ("dp_0", "dp_1", "dp_2", "slot", "hid"),
    )
    states = P("slot", None, "hid", DP)
    rows = P(DP, None)
    in_specs = (states,) * 3 + (rows,) * 7 + (P(), P())
    out_specs = (states,) * 3 + (P(DP, ("slot", "hid")),)
    return jax.shard_map(
        per_device, mesh=split, in_specs=in_specs, out_specs=out_specs, check_vma=False
    )
```

```python
import jax
import jax.numpy as jnp
from jax import lax
from jax.experimental import pallas as pl
from jax.experimental.pallas import tpu as pltpu
from jax.sharding import Mesh
from jax.sharding import PartitionSpec as P

DP = ("dp_0", "dp_1", "dp_2")
BF = jnp.bfloat16
F32 = jnp.float32

learn_rate = 0.001
beta_one = 0.9
beta_two = 0.95
epsilon = 1e-08
decay_rate = 0.1

TILE = 512
CHUNKS = 2
VMEM_BYTES = 32 * 2**20


def from_ahead(x, axis, step):
    n = lax.axis_size(axis)
    return lax.ppermute(x, axis, [((i + step) % n, i) for i in range(n)])


def swapped(x):
    return from_ahead(x, "dp_2", 1)


def to_ahead(x, axis, step):
    return from_ahead(x, axis, -step)


def together(*values):
    return lax.optimization_barrier(values)


def rows_by(left, right):
    return lax.dot_general(
        left, right, (((1,), (1,)), ((), ())), preferred_element_type=F32
    )


def kernel_params(count=1):
    return pltpu.CompilerParams(
        dimension_semantics=("arbitrary",) * count, vmem_limit_bytes=VMEM_BYTES
    )


def whole(shape):
    return pl.BlockSpec(shape, lambda i, s: (0,) * len(shape))


def column_block(index, cols):
    return pl.ds(pl.multiple_of(index * cols, cols), cols)


def first_half(where, far, tokens, scaled_grad, weights, partial=None):
    count, width = tokens.shape
    chips, rows, cols = weights.shape
    units = rows // 3
    last = partial is not None

    def body(where_ref, t, g, pieces, *refs):
        out, held = refs[-2:]

        @pl.when(pl.program_id(0) == 0)
        def _():
            for step in range(chips):
                held[:, column_block((where_ref[1] + step) % chips, cols)] = pieces[step]

        both = rows_by(held[: 2 * units, :], t[...])
        d_act = rows_by(held[2 * units :, :], g[...])
        if not last:
            out[: 2 * units, :] = both
            out[2 * units :, :] = d_act
            return
        gate = both[:units] + refs[0][:units, :]
        up = both[units:] + refs[0][units : 2 * units, :]
        d_act = d_act + refs[0][2 * units :, :]
        sig = jax.nn.sigmoid(gate)
        swish = gate * sig
        out[:units, :] = (d_act * up * sig * (1.0 + gate * (1.0 - sig))).astype(BF)
        out[units : 2 * units, :] = (d_act * swish).astype(BF)
        out[2 * units :, :] = (swish * up).astype(BF)

    token_block = pl.BlockSpec((TILE, width // 2), lambda i, s: (i, 1 - s[0] if far else s[0]))
    by_token = pl.BlockSpec((rows, TILE), lambda i, s: (0, i))
    return pl.pallas_call(
        body,
        grid_spec=pltpu.PrefetchScalarGridSpec(
            num_scalar_prefetch=1,
            grid=(count // TILE,),
            in_specs=[token_block, token_block, whole(weights.shape)] + [by_token] * last,
            out_specs=by_token,
            scratch_shapes=[pltpu.VMEM((rows, width // 2), BF)],
        ),
        out_shape=jax.ShapeDtypeStruct((rows, count), BF if last else F32),
        compiler_params=kernel_params(),
        cost_estimate=pl.CostEstimate(
            flops=count * width * rows, bytes_accessed=8 * 2**20, transcendentals=last * count * units
        ),
    )(where, tokens, scaled_grad, weights, *([partial] if last else []))


def gradient_half(where, tokens, cotangent, factors):
    rows, count = factors[0].shape
    units = rows // 3
    chips, cols = 4, tokens[0].shape[1] // 8

    def body(where_ref, t_a, t_b, g_a, g_b, a_ref, b_ref, out):
        out[0, : 2 * units, :] = (
            jnp.dot(a_ref[: 2 * units, :], t_a[...], preferred_element_type=F32)
            + jnp.dot(b_ref[: 2 * units, :], t_b[...], preferred_element_type=F32)
        ).astype(BF)
        out[0, 2 * units :, :] = (
            jnp.dot(a_ref[2 * units :, :], g_a[...], preferred_element_type=F32)
            + jnp.dot(b_ref[2 * units :, :], g_b[...], preferred_element_type=F32)
        ).astype(BF)

    block = pl.BlockSpec((count, cols), lambda i, s: (0, s[0] * chips + (s[1] + i) % chips))
    return pl.pallas_call(
        body,
        grid_spec=pltpu.PrefetchScalarGridSpec(
            num_scalar_prefetch=1,
            grid=(chips,),
            in_specs=[block] * 4 + [whole((rows, count))] * 2,
            out_specs=pl.BlockSpec((1, rows, cols), lambda i, s: (i, 0, 0)),
        ),
        out_shape=jax.ShapeDtypeStruct((chips, rows, cols), BF),
        compiler_params=kernel_params(),
        cost_estimate=pl.CostEstimate(
            flops=4 * count * rows * chips * cols, bytes_accessed=12 * 2**20, transcendentals=0
        ),
    )(where, *tokens, *cotangent, *factors)


def down_blocks(where_ref, chips):
    for half in range(2):
        for step in range(chips):
            z_half = 1 - where_ref[0] if half else where_ref[0]
            x = (where_ref[1] + step) % chips
            ahead = (z_half * 2 + x // 2 + 4 - where_ref[2]) % 4
            for core in range(2):
                yield half, step, core, ahead, (x % 2 * 2 + core + 4 - where_ref[3]) % 4


def held_up(where_ref, pieces, held):
    chips, rows, cols = pieces[0].shape
    units = rows // 3
    for step in range(chips):
        span = column_block((where_ref[1] + step) % chips, cols)
        for e in range(2):
            for kind in range(2):
                start = (kind * 2 + e) * units
                held[start : start + units, span] = pieces[e][step, kind * units : (kind + 1) * units, :]


def second_near(where, tokens, own, other):
    count, width = tokens.shape
    chips, rows, cols = own.shape
    units = rows // 3

    def body(where_ref, t, own_ref, oth_ref, out, held):
        @pl.when(pl.program_id(0) == 0)
        def _():
            held_up(where_ref, (own_ref, oth_ref), held)

        out[...] = rows_by(t[...], held[...])

    return pl.pallas_call(
        body,
        grid_spec=pltpu.PrefetchScalarGridSpec(
            num_scalar_prefetch=1,
            grid=(count // TILE,),
            in_specs=[pl.BlockSpec((TILE, width // 2), lambda i, s: (i, s[0]))]
            + [whole(own.shape)] * 2,
            out_specs=pl.BlockSpec((TILE, 4 * units), lambda i, s: (i, 0)),
            scratch_shapes=[pltpu.VMEM((4 * units, width // 2), BF)],
        ),
        out_shape=jax.ShapeDtypeStruct((count, 4 * units), F32),
        compiler_params=kernel_params(),
        cost_estimate=pl.CostEstimate(
            flops=4 * count * width * units, bytes_accessed=8 * 2**20, transcendentals=0
        ),
    )(where, tokens, own, other)


def second_hidden(where, tokens, scaling, partial, weights):
    count, width = tokens.shape
    chips, rows, cols = weights[0].shape
    units = rows // 3
    lanes = cols // 2

    def body(where_ref, t, s_ref, part, own_n, oth_n, own_f, oth_f, mix_out, share_out, held, down):
        @pl.when(pl.program_id(0) == 0)
        def _():
            held_up(where_ref, (own_f, oth_f), held)
            pieces = ((own_n, oth_n), (own_f, oth_f))
            for half, step, core, ahead, place in down_blocks(where_ref, chips):

                @pl.when(ahead == 2)
                def _():
                    first = 2 * units if half else 0
                    for e in range(2):
                        down[e * units : (e + 1) * units, column_block(place, lanes)] = pieces[half][e][
                            step, first : first + units, core * lanes : (core + 1) * lanes
                        ]

        both = rows_by(t[...], held[...]) + part[...]
        gate = both[:, : 2 * units]
        unit = lax.broadcasted_iota(jnp.int32, (TILE, 2 * units), 1)
        scale = jnp.where(unit < units, s_ref[:, 0:1], s_ref[:, 1:2])
        mixed = (scale * gate * jax.nn.sigmoid(gate) * both[:, 2 * units :]).astype(BF)
        mix_out[...] = mixed
        share_out[...] = jnp.dot(mixed, down[...], preferred_element_type=F32).astype(BF)

    def by_token(size):
        return pl.BlockSpec((TILE, size), lambda i, s: (i, 0))

    return pl.pallas_call(
        body,
        grid_spec=pltpu.PrefetchScalarGridSpec(
            num_scalar_prefetch=1,
            grid=(count // TILE,),
            in_specs=[pl.BlockSpec((TILE, width // 2), lambda i, s: (i, 1 - s[0]))]
            + [by_token(2), by_token(4 * units)]
            + [pl.BlockSpec((chips, units, cols), lambda i, s: (0, 2, 0))] * 2
            + [whole(weights[0].shape)] * 2,
            out_specs=[by_token(2 * units), by_token(4 * lanes)],
            scratch_shapes=[
                pltpu.VMEM((4 * units, width // 2), BF),
                pltpu.VMEM((2 * units, 4 * lanes), BF),
            ],
        ),
        out_shape=[
            jax.ShapeDtypeStruct((count, 2 * units), BF),
            jax.ShapeDtypeStruct((count, 4 * lanes), BF),
        ],
        compiler_params=kernel_params(),
        cost_estimate=pl.CostEstimate(
            flops=5 * count * width * units, bytes_accessed=10 * 2**20, transcendentals=2 * count * units
        ),
    )(where, tokens, scaling, partial, *weights)


def second_shares(where, mixed, weights, parts):
    count = mixed.shape[0] // parts
    chips, rows, cols = weights[0].shape
    units = rows // 3
    lanes = cols // 2
    steps = (1, 3, 0)

    def body(where_ref, mix_ref, own_n, oth_n, own_f, oth_f, *refs):
        outs, held = refs[:-1], refs[-1]
        pieces = ((own_n, oth_n), (own_f, oth_f))
        for half, step, core, ahead, place in down_blocks(where_ref, chips):
            for e in range(2):
                held[e * units : (e + 1) * units, column_block(ahead * 4 + place, lanes)] = pieces[half][e][
                    step, :, core * lanes : (core + 1) * lanes
                ]
        for part in range(parts):
            for place, step in enumerate(steps):
                outs[part * len(steps) + place][...] = jnp.dot(
                    mix_ref[part * count : (part + 1) * count, :],
                    held[:, step * 4 * lanes : (step + 1) * 4 * lanes],
                    preferred_element_type=F32,
                ).astype(BF)

    down = pl.BlockSpec((chips, units, cols), lambda i, s: (0, 2, 0))
    shares = pl.pallas_call(
        body,
        grid_spec=pltpu.PrefetchScalarGridSpec(
            num_scalar_prefetch=1,
            grid=(1,),
            in_specs=[whole(mixed.shape)] + [down] * 4,
            out_specs=[whole((count, 2 * cols))] * (len(steps) * parts),
            scratch_shapes=[pltpu.VMEM((2 * units, 2 * chips * cols), BF)],
        ),
        out_shape=[jax.ShapeDtypeStruct((count, 2 * cols), BF)] * (len(steps) * parts),
        compiler_params=kernel_params(),
        cost_estimate=pl.CostEstimate(
            flops=6 * count * parts * units * chips * cols * 2, bytes_accessed=6 * 2**20, transcendentals=0
        ),
    )(where, mixed, *weights)
    return [
        dict(zip(steps, shares[part * len(steps) : (part + 1) * len(steps)])) for part in range(parts)
    ]


def along_x(piece):
    return [piece] + [from_ahead(piece, "dp_1", step) for step in (1, 2, 3)]


def adamw_update(master, moment_a, moment_b, grad_sum):
    new_a = beta_one * moment_a + (1.0 - beta_one) * grad_sum
    new_b = beta_two * moment_b + (1.0 - beta_two) * grad_sum * grad_sum
    fixed_a = new_a / (1.0 - beta_one**10)
    fixed_b = new_b / (1.0 - beta_two**10)
    new_master = master - learn_rate * (
        fixed_a / (jnp.sqrt(fixed_b) + epsilon) + decay_rate * master
    )
    return (new_master, new_a, new_b)


def moved_states(mine, states, grads):
    _, kinds, local, rows, width = states.shape

    def body(mine_ref, old, grad, *outs):
        new = adamw_update(old[0, 0, 0], old[0, 1, 0], old[0, 2, 0], grad[0, 0].astype(F32))
        for value, out in zip(new, outs):
            out[0] = value

    return pl.pallas_call(
        body,
        grid_spec=pltpu.PrefetchScalarGridSpec(
            num_scalar_prefetch=1,
            grid=(local,),
            in_specs=[
                pl.BlockSpec((1, kinds, 1, rows, width), lambda i, s: (s[i] // local, 0, s[i] % local, 0, 0)),
                pl.BlockSpec((1, 1, rows, width), lambda i, s: (s[i] // local, s[i] % local, 0, 0)),
            ],
            out_specs=[pl.BlockSpec((1, rows, width), lambda i, s: (i, 0, 0))] * kinds,
        ),
        out_shape=[jax.ShapeDtypeStruct((local, rows, width), F32)] * kinds,
        compiler_params=kernel_params(),
        cost_estimate=pl.CostEstimate(
            flops=40 * local * rows * width, bytes_accessed=4 * 2**20, transcendentals=2 * local * rows * width
        ),
    )(mine, states, grads)


def coefficients(routes, probs, expert_ids):
    matches = routes[:, :, None] == expert_ids[None, None, :]
    return jnp.sum(jnp.where(matches, probs[:, :, None], 0.0), axis=1)


def per_device(
    master_weights,
    first_moment,
    second_moment,
    tokens_one,
    grad_out,
    route_one,
    prob_one,
    tokens_two,
    route_two,
    prob_two,
    old_order,
    new_order,
):
    local_count, kinds, units, width = master_weights.shape
    slot = lax.axis_index("slot")
    hid = lax.axis_index("hid")
    z_half = lax.axis_index("dp_0")
    chip_x = lax.axis_index("dp_1")
    is_zero = lax.axis_index("dp_2") == 0
    where = jnp.stack([z_half, chip_x, slot, hid]).astype(jnp.int32)
    where_far = jnp.stack([1 - z_half, chip_x, slot, hid]).astype(jnp.int32)
    offset = slot * local_count
    held_ids = lax.dynamic_slice_in_dim(old_order, offset, local_count)
    ids_here = jnp.where(is_zero, held_ids, held_ids[::-1])
    rows = kinds * units

    def own_and_other(x):
        return jnp.where(is_zero, x[0], x[1]), jnp.where(is_zero, x[1], x[0])

    def in_order(mine, sibling, axis):
        return jnp.where(
            is_zero,
            jnp.concatenate([mine, sibling], axis=axis),
            jnp.concatenate([sibling, mine], axis=axis),
        )

    bf_own, bf_other = own_and_other(
        master_weights.astype(BF).reshape(local_count, rows, width)
    )
    scaling_one = coefficients(route_one, prob_one, ids_here)
    scaled_own, scaled_other = [
        (scaling_one[:, e : e + 1] * grad_out.astype(F32)).astype(BF) for e in range(2)
    ]
    piece, tokens_ready = together(in_order(bf_own, swapped(bf_other), 1), tokens_one)
    far_piece, near, sibling_tokens, scaled_other = together(
        from_ahead(piece, "dp_0", 1), along_x(piece), swapped(tokens_ready), scaled_other
    )
    tokens = (tokens_one, sibling_tokens)
    cotangent = (scaled_own, swapped(scaled_other))

    states = jnp.stack([master_weights, first_moment, second_moment])
    states = states.reshape(3, local_count, rows, width)
    all_states = lax.all_gather(states, "slot")
    st_own, st_other = own_and_other(states.swapaxes(0, 1))
    pair_states = in_order(st_own, swapped(st_other), 2)

    near = jnp.stack(near)
    far, partials = together(
        along_x(far_piece),
        [first_half(where, False, tokens[core], cotangent[core], near) for core in range(2)],
    )
    far = jnp.stack(far)
    factors = [
        first_half(where, True, tokens[core], cotangent[core], far, partials[core])
        for core in range(2)
    ]

    def chip_sum(place):
        grads = gradient_half(place, tokens, cotangent, factors)
        total = grads[0].astype(F32)
        for step in (2, 1, 3):
            total = total + to_ahead(grads[step], "dp_1", step).astype(F32)
        return total

    from_far = from_ahead(chip_sum(where_far).astype(BF), "dp_0", 1)
    pair_grads = (chip_sum(where) + from_far.astype(F32)).astype(BF)

    new_master = adamw_update(*pair_states, pair_grads.astype(F32))[0]
    next_piece = new_master.astype(BF)
    keep = jnp.where(is_zero, pair_grads[:, :width], pair_grads[:, width:])
    give = jnp.where(is_zero, pair_grads[:, width:], pair_grads[:, :width])
    next_far, next_near, grads = together(
        from_ahead(next_piece, "dp_0", 1),
        along_x(next_piece),
        in_order(keep[None], swapped(give)[None], 0),
    )
    grads, all_states = together(grads, all_states)
    all_grads = lax.all_gather(grads, "slot")
    next_near = jnp.stack(next_near)
    other_near = swapped(next_near)
    next_far, partial = together(
        along_x(next_far), second_near(where, tokens_two, next_near, other_near)
    )
    next_far = jnp.stack(next_far)
    next_weights = (next_near, other_near, next_far, swapped(next_far))

    positions = jnp.arange(old_order.shape[0], dtype=jnp.int32)
    source = jnp.sum(
        jnp.where(old_order[None, :] == new_order[:, None], positions[None, :], 0), axis=1
    )
    mine = lax.dynamic_slice_in_dim(source, offset, local_count)

    scaling_two = coefficients(route_two, prob_two, ids_here)
    (mixed, opposite), all_grads = together(
        second_hidden(where, tokens_two, scaling_two, partial, next_weights), all_grads
    )
    from_opposite = to_ahead(opposite, "slot", 2)
    mine, opposite = together(mine, opposite)
    moved = [
        x.reshape(master_weights.shape) for x in moved_states(mine, all_states, all_grads)
    ]
    shares = second_shares(where, mixed, next_weights, CHUNKS)
    count = tokens_two.shape[0] // CHUNKS
    outs = []
    for chunk, share in enumerate(shares):
        came = [to_ahead(share[step], "slot", step) for step in (1, 3)]
        if chunk == 0:
            came, moved = together(came, moved)
        else:
            came, outs = together(came, outs)
        total = share[0].astype(F32)
        for value in (from_opposite[chunk * count : (chunk + 1) * count], *came):
            total = total + value.astype(F32)
        result = total[:, :width]
        for step in (1, 2, 3):
            part = total[:, step * width : (step + 1) * width].astype(BF)
            result = result + to_ahead(part, "hid", step).astype(F32)
        outs.append(result.astype(BF))
    return (*moved, jnp.concatenate(outs, axis=0))


def solution(mesh):
    split = Mesh(
        mesh.devices.reshape(2, 4, 2, mesh.shape["slot"], mesh.shape["hid"]),
        ("dp_0", "dp_1", "dp_2", "slot", "hid"),
    )
    states = P("slot", None, "hid", DP)
    rows = P(DP, None)
    in_specs = (states,) * 3 + (rows,) * 7 + (P(), P())
    out_specs = (states,) * 3 + (P(DP, ("slot", "hid")),)
    return jax.shard_map(
        per_device, mesh=split, in_specs=in_specs, out_specs=out_specs, check_vma=False
    )
```
